32 devices in a mesh: region: 4 (over y, core), dev: 8 (over z, x).
Axes of the slice: x: 2, y: 2, z: 4, core: 2. Of those that a mesh axis runs over, the one named last changes fastest.
Arguments:
- feats: bfloat16 [65536, 128], P(('region', 'dev')), may hold values from -6 to 6
- neighbours: int32 [27, 65536], P(None, ('region', 'dev')), may hold values from -1 to 2559, as said below
- send_rows: int32 [32, 512], P(('region', 'dev')), may hold values from 0 to 2047
- patch_ids: int32 [65536], P(('region', 'dev')), may hold values from 0 to 127, never falling along the last dimension, each value on 1 to 1024 neighbouring positions
- conv_weight: bfloat16 [27, 128, 128], replicated, may hold values from -0.109375 to 0.109375
- norm1_gain: float32 [128], replicated, may hold values from 0.25 to 1.75
- query_weight: bfloat16 [128, 128], replicated
- key_weight: bfloat16 [128, 128], replicated
- value_weight: bfloat16 [128, 128], replicated, may hold values from -0.5 to 0.5
- out_weight: bfloat16 [128, 128], replicated, may hold values from -0.5 to 0.5
- norm2_gain: float32 [128], replicated, may hold values from 0.25 to 1.75
- up_weight: bfloat16 [128, 512], replicated, may hold values from -0.5 to 0.5
- down_weight: bfloat16 [512, 128], replicated, may hold values from -0.25 to 0.25
Outputs:
- block_out: bfloat16 [65536, 128], P(('region', 'dev'))
The draws below stay inside these ranges and needn't reach their ends.
Inputs may be any that keep to these rules, and one draw needn't show every extreme that they name: `neighbours`: the offset in the middle of the kernel names the voxel itself; other entries are -1, a row of the own device, or 2048 + p * 64 + s for slot s of what device p of the same region sends. `send_rows`: row e, column q * 64 + s names the row of device e that goes into slot s of its message to device q of its region. `patch_ids`: Non-decreasing along the curve; each patch has 1 to 1024 consecutive voxels, one exactly 1024.
All inputs are finite; a program needn't handle non-finite values.
Results may differ from the reference program's by a relative error of at most 0.018.
Values may be sent and summed in bfloat16 or wider, within the bound.
A program may use at most 128 MiB of HBM per device.

```python
import math
import jax
import jax.numpy as jnp
import numpy as np
from jax import lax

C = 128
HEADS = 8
HID = 512
PMAX = 1024
TAPS = 27
VOX_DEV = 2048
CAP = 64
VOX = 65536
N_DEV = 8
DEVICES = 32


def draw_neighbours(key, part):
    columns = jnp.arange(VOX, dtype=jnp.int32)
    position = columns % VOX_DEV
    kinds = jax.random.randint(jax.random.fold_in(key, 1), (TAPS, VOX), 0, 20)
    near_rows = jnp.clip(position[None, :] + jax.random.randint(jax.random.fold_in(key, 2), (TAPS, VOX), -96, 97), 0, VOX_DEV - 1)
    far_rows = VOX_DEV + jax.random.randint(jax.random.fold_in(key, 3), (TAPS, VOX), 0, N_DEV * CAP)
    entries = jnp.where(kinds < 6, -1, jnp.where(kinds < 14, near_rows, far_rows))
    middle = (jnp.arange(TAPS, dtype=jnp.int32) == TAPS // 2)[:, None]
    return jnp.where(middle, position[None, :], entries).astype(jnp.int32)


def draw_query_weight(key, part):
    shared = jax.random.normal(jax.random.fold_in(key, 11), (C, C), jnp.float32)
    return (shared * C ** (-0.5)).astype(jnp.bfloat16)


def draw_key_weight(key, part):
    own = jax.random.normal(jax.random.fold_in(key, 12), (C, C), jnp.float32)
    return (own * C ** (-0.5)).astype(jnp.bfloat16)


def set_ends(drawn, key, least, high):
    spot = [jax.random.randint(jax.random.fold_in(key, axis), (), 0, length) for axis, length in enumerate(drawn.shape)]
    longest = drawn.shape.index(max(drawn.shape))
    next_to = spot[:longest] + [(spot[longest] + 1) % drawn.shape[longest]] + spot[longest + 1:]
    return drawn.at[tuple(spot)].set(least).at[tuple(next_to)].set(high)


def block_levels(stream_key, extent, shards, least, largest):
    factor_of = 1.0
    for dim, shards_of in shards:
        heights = jax.random.uniform(jax.random.fold_in(jax.random.fold_in(stream_key, 6), dim), (shards_of,), jnp.float32, least / len(shards), largest / len(shards))
        factor_of = factor_of * jnp.repeat(jnp.exp(heights), extent[dim] // shards_of).reshape((-1,) + (1,) * (len(extent) - 1 - dim))
    return factor_of


def length_profile(count, total, reach, skew):
    loads = [(1 << 20) // math.isqrt(standing ** skew) + 1 for standing in range(2, count + 1)]
    rest, given = total - reach - (count - 1), [1] * (count - 1)
    while rest > 0:
        movable = [i for i in range(count - 1) if given[i] < reach]
        mass, budget = sum([loads[i] for i in movable]), rest
        for i in movable:
            extra = min(reach - given[i], max(1, budget * loads[i] // mass), rest)
            given[i] = given[i] + extra
            rest = rest - extra
    return np.array([reach] + given)


def ragged_sizes(rng, count, total, most, lean):
    if count == 2:
        one = jax.random.randint(rng, (), max(1, total - most), min(most, total - 1) + 1)
        return jnp.stack([one, total - one])
    sizes = jnp.asarray(length_profile(count, total, most, lean), jnp.int32)
    twos = (count - 1) // 2
    giver, sink = sizes[1:1 + 2 * twos:2], sizes[2:2 + 2 * twos:2]
    room = jnp.minimum(giver - 1, most - sink)
    passed = jax.random.randint(jax.random.fold_in(rng, 1), (twos,), 0, 1 << 20) % (room + 1)
    sizes = sizes.at[1:1 + 2 * twos:2].set(giver - passed).at[2:2 + 2 * twos:2].set(sink + passed)
    return sizes[jax.random.permutation(jax.random.fold_in(rng, 2), count)]


def gaussian(rng, extent, scale, limit, split=(), kind=jnp.bfloat16):
    drawn = jax.random.normal(rng, extent, jnp.float32) * scale
    if len(split) > 0:
        drawn = block_levels(rng, extent, split, -0.22, 0.18) * drawn
    return jnp.clip(drawn, min=-limit, max=limit).astype(kind)


def setup_inputs(seed: int = 0) -> dict:
    seeds = jax.random.split(jax.random.key(seed), 14)
    return {
        "feats": gaussian(seeds[0], (VOX, C), 1.0, 6.0, ((0, 32),)),
        "neighbours": draw_neighbours(jax.random.fold_in(seeds[13], 71), 0),
        "send_rows": set_ends(jax.random.randint(seeds[2], (DEVICES, N_DEV * CAP), 0, VOX_DEV), jax.random.fold_in(seeds[2], 1), 0, VOX_DEV - 1).astype(jnp.int32),
        "patch_ids": jnp.searchsorted(jnp.cumsum(ragged_sizes(seeds[3], 2 * VOX // PMAX, VOX, PMAX, 0)), jnp.arange(VOX), side="right").astype(jnp.int32),
        "conv_weight": gaussian(seeds[4], (TAPS, C, C), (TAPS * C) ** -0.5, 0.109375),
        "norm1_gain": jnp.clip(1.0 + 0.15 * jax.random.normal(seeds[5], (C,), jnp.float32), 0.25, 1.75),
        "query_weight": draw_query_weight(jax.random.fold_in(seeds[13], 71), 0),
        "key_weight": draw_key_weight(jax.random.fold_in(seeds[13], 71), 0),
        "value_weight": gaussian(seeds[8], (C, C), C ** -0.5, 0.5),
        "out_weight": gaussian(seeds[9], (C, C), C ** -0.5, 0.5),
        "norm2_gain": jnp.clip(1.0 + 0.15 * jax.random.normal(seeds[10], (C,), jnp.float32), 0.25, 1.75),
        "up_weight": gaussian(seeds[11], (C, HID), C ** -0.5, 0.5),
        "down_weight": gaussian(seeds[12], (HID, C), HID ** -0.5, 0.25),
    }


def layer_norm(inputs, norm_gain):
    inputs = inputs.astype(jnp.float32)
    center = inputs - lax.optimization_barrier(jnp.mean(inputs, axis=-1, keepdims=True))
    spread = lax.optimization_barrier(jnp.mean(center * center, axis=-1, keepdims=True))
    return center * lax.rsqrt(spread + 1e-05) * norm_gain.astype(jnp.float32)

def attend_block(queries, query_ids, keys, values, key_ids):
    count_q = queries.shape[0]
    count_k = keys.shape[0]
    head_size = C // HEADS
    query_heads = queries.astype(jnp.float32).reshape(count_q, HEADS, head_size)
    key_heads = keys.astype(jnp.float32).reshape(count_k, HEADS, head_size)
    value_heads = values.astype(jnp.float32).reshape(count_k, HEADS, head_size)
    scores = jnp.einsum('qhd,khd->hqk', query_heads, key_heads) * head_size ** (-0.5)
    same_patch = (query_ids[:, None] == key_ids[None, :])[None, :, :]
    scores = jnp.where(same_patch, scores, -1e+30)
    highest = lax.optimization_barrier(jnp.max(scores, axis=-1, keepdims=True))
    expo = jnp.where(same_patch, jnp.exp(scores - highest), 0.0)
    totals = lax.optimization_barrier(jnp.sum(expo, axis=-1, keepdims=True))
    weights = (expo / totals).astype(jnp.bfloat16)
    mixed_heads = jnp.einsum('hqk,khd->qhd', weights.astype(jnp.float32), value_heads)
    return mixed_heads.reshape(count_q, C).astype(jnp.bfloat16)

def reference(feats, neighbours, send_rows, patch_ids, conv_weight, norm1_gain, query_weight, key_weight, value_weight, out_weight, norm2_gain, up_weight, down_weight):
    columns = jnp.arange(VOX, dtype=jnp.int32)
    owner = columns // VOX_DEV
    region_first = owner // N_DEV * N_DEV
    dest_slot = owner % N_DEV * CAP
    flat_send = send_rows.reshape(-1)

    def global_index(entries):
        remote = jnp.maximum(entries - VOX_DEV, 0)
        source = region_first + remote // CAP
        picked = jnp.take(flat_send, source * (N_DEV * CAP) + dest_slot + remote % CAP)
        far_index = source * VOX_DEV + picked
        near_index = owner * VOX_DEV + jnp.clip(entries, 0, VOX_DEV - 1)
        return jnp.where(entries >= VOX_DEV, far_index, near_index).astype(jnp.int32)

    def one_tap(tap_index, total):
        entries = lax.dynamic_index_in_dim(neighbours, tap_index, 0, keepdims=False)
        gathered = jnp.take(feats, global_index(entries), axis=0)
        gathered = jnp.where((entries >= 0)[:, None], gathered, jnp.zeros_like(gathered))
        kernel = lax.dynamic_index_in_dim(conv_weight, tap_index, 0, keepdims=False)
        return total + jnp.dot(gathered, kernel, preferred_element_type=jnp.float32)
    conv_sum = lax.fori_loop(0, TAPS, one_tap, jnp.zeros((VOX, C), jnp.float32))
    after_conv = (feats.astype(jnp.float32) + conv_sum).astype(jnp.bfloat16)
    normed = layer_norm(after_conv, norm1_gain).astype(jnp.bfloat16)
    queries = jnp.dot(normed, query_weight, preferred_element_type=jnp.float32).astype(jnp.bfloat16)
    keys = jnp.dot(normed, key_weight, preferred_element_type=jnp.float32).astype(jnp.bfloat16)
    values = jnp.dot(normed, value_weight, preferred_element_type=jnp.float32).astype(jnp.bfloat16)
    padded_keys = jnp.pad(keys, ((PMAX, PMAX), (0, 0)))
    padded_values = jnp.pad(values, ((PMAX, PMAX), (0, 0)))
    padded_ids = jnp.pad(patch_ids, (PMAX, PMAX), constant_values=-1)
    block_rows = min(512, VOX_DEV)
    window = block_rows + 2 * PMAX

    def one_block(block_index):
        offset = block_index * block_rows
        query_part = lax.dynamic_slice_in_dim(queries, offset, block_rows, 0)
        query_ids = lax.dynamic_slice_in_dim(patch_ids, offset, block_rows, 0)
        key_part = lax.dynamic_slice_in_dim(padded_keys, offset, window, 0)
        value_part = lax.dynamic_slice_in_dim(padded_values, offset, window, 0)
        key_ids = lax.dynamic_slice_in_dim(padded_ids, offset, window, 0)
        return attend_block(query_part, query_ids, key_part, value_part, key_ids)
    attended = lax.map(one_block, jnp.arange(VOX // block_rows, dtype=jnp.int32)).reshape(VOX, C)
    after_attn = (after_conv.astype(jnp.float32) + jnp.dot(attended, out_weight, preferred_element_type=jnp.float32)).astype(jnp.bfloat16)
    normed2 = layer_norm(after_attn, norm2_gain).astype(jnp.bfloat16)
    hidden = jax.nn.gelu(jnp.dot(normed2, up_weight, preferred_element_type=jnp.float32), approximate=False).astype(jnp.bfloat16)
    block_out = (after_attn.astype(jnp.float32) + jnp.dot(hidden, down_weight, preferred_element_type=jnp.float32)).astype(jnp.bfloat16)
    return block_out
```

```python
import functools
import math

import jax
import jax.numpy as jnp
from jax import lax
from jax.experimental import pallas as pl
from jax.experimental.pallas import tpu as pltpu
from jax.sharding import PartitionSpec as P

HEADS = 8
PMAX = 1024
BLOCK = 256
LEAD = 8
VROWS = 32
FAR = -1e30
F32 = jnp.float32
BF16 = jnp.bfloat16


def shifted(block, axis, distance):
    devices = range(lax.axis_size(axis))
    route = [(i - distance, i) for i in devices if i - distance in devices]
    return lax.ppermute(block, axis, route)


def layer_norm(inputs, norm_gain):
    inputs = inputs.astype(F32)
    center = inputs - jnp.mean(inputs, axis=-1, keepdims=True)
    spread = jnp.mean(center * center, axis=-1, keepdims=True)
    return (center * lax.rsqrt(spread + 1e-05) * norm_gain).astype(BF16)


def dot(a, b):
    return jnp.dot(a, b, preferred_element_type=F32)


def conv_kernel(nb_ref, feats_ref, inc_ref, w_ref, out_ref, tab, gath):
    step = pl.program_id(0)
    rows, channels = feats_ref.shape
    far = inc_ref.shape[0]
    taps, block = nb_ref.shape
    middle = taps // 2

    @pl.when(step == 0)
    def _():
        tab[0:LEAD, :] = jnp.zeros((LEAD, channels), F32)
        tab[LEAD : LEAD + rows, :] = feats_ref[...].astype(F32)
        tab[LEAD + rows : LEAD + rows + far, :] = inc_ref[...].astype(F32)

    def group(index, carry):
        base = pl.multiple_of(index * 8, 8)
        for tap in range(taps):
            if tap == middle:
                continue
            for j in range(8):
                row = nb_ref[tap, base + j] + LEAD
                gath[tap, pl.ds(base + j, 1), :] = tab[pl.ds(row, 1), :]
        return carry

    lax.fori_loop(0, block // 8, group, 0)
    own = tab[pl.ds(pl.multiple_of(step * block + LEAD, 8), block), :]
    gath[middle] = own
    wide = jnp.concatenate([gath[tap].astype(BF16) for tap in range(taps)], axis=1)
    total = dot(wide, w_ref[...])
    out_ref[...] = (own + total).astype(BF16)


def conv(feats, incoming, neighbours, conv_weight):
    rows, channels = feats.shape
    taps = neighbours.shape[0]
    far = incoming.shape[0]
    block = min(BLOCK, rows)
    return pl.pallas_call(
        conv_kernel,
        grid=(rows // block,),
        out_shape=jax.ShapeDtypeStruct((rows, channels), BF16),
        in_specs=[
            pl.BlockSpec((taps, block), lambda i: (0, i), memory_space=pltpu.SMEM),
            pl.BlockSpec(memory_space=pltpu.VMEM),
            pl.BlockSpec(memory_space=pltpu.VMEM),
            pl.BlockSpec(memory_space=pltpu.VMEM),
        ],
        out_specs=pl.BlockSpec((block, channels), lambda i: (i, 0)),
        scratch_shapes=[
            pltpu.VMEM((LEAD + rows + far, channels), F32),
            pltpu.VMEM((taps, block, channels), F32),
        ],
        compiler_params=pltpu.CompilerParams(vmem_limit_bytes=48 * 2**20),
        name="conv",
    )(neighbours, feats, incoming, conv_weight.reshape(taps * channels, channels))


def attn_kernel(
    ids_ref, codes_ref, mid_ref, before_ref, after_ref,
    g1_ref, wq_ref, wk_ref, wv_ref, wo_ref, g2_ref, up_ref, down_ref,
    out_ref, kbuf, vbuf, kcode, qz, bias, mbuf, acc,
):
    rows, channels = mid_ref.shape
    head = channels // HEADS
    edge = before_ref.shape[0]
    blocks = (rows + 2 * edge) // BLOCK
    lanes = codes_ref.shape[1]
    g1 = g1_ref[...]

    def keys_values(normed, slot):
        kbuf[pl.ds(pl.multiple_of(slot * BLOCK, BLOCK), BLOCK), :] = dot(normed, wk_ref[...]).astype(BF16)
        vt = dot(normed, wv_ref[...]).T.astype(BF16)
        vv = vt.reshape(HEADS, head, BLOCK)
        ones = jnp.ones((HEADS, VROWS - head, BLOCK), BF16)
        vbuf[slot] = jnp.concatenate([vv, ones], axis=1).reshape(HEADS * VROWS, BLOCK)

    def side(ref, first):
        def one(i, carry):
            part = ref[pl.ds(pl.multiple_of(i * BLOCK, BLOCK), BLOCK), :]
            keys_values(layer_norm(part, g1), first + i)
            return carry
        lax.fori_loop(0, ref.shape[0] // BLOCK, one, 0)

    side(before_ref, 0)
    side(mid_ref, edge // BLOCK)
    side(after_ref, (edge + rows) // BLOCK)

    def code_column(i, carry):
        line = codes_ref[pl.ds(i, 1), :]
        kcode[pl.ds(pl.multiple_of(i * lanes, lanes), lanes), :] = jnp.broadcast_to(line, (lanes, lanes)).T
        return carry

    lax.fori_loop(0, codes_ref.shape[0], code_column, 0)
    all_codes = codes_ref[...]

    def query_block(i, carry):
        start = pl.multiple_of(i * BLOCK, BLOCK)
        mine = mid_ref[pl.ds(start, BLOCK), :]
        query = dot(layer_norm(mine, g1), wq_ref[...]) * (head ** (-0.5) * math.log2(math.e))
        qt = query.T.astype(BF16)
        qz[...] = jnp.zeros(qz.shape, BF16)
        for h in range(HEADS):
            qz[h, h * head : (h + 1) * head, :] = qt[h * head : (h + 1) * head, :]
        first = ids_ref[0, start].astype(F32) + 1.0
        last = ids_ref[0, start + BLOCK - 1].astype(F32) + 1.0
        low = jnp.sum(jnp.where(all_codes < first, 1.0, 0.0)).astype(jnp.int32)
        high = jnp.sum(jnp.where(all_codes <= last, 1.0, 0.0)).astype(jnp.int32)
        mbuf[...] = jnp.full(mbuf.shape, FAR, F32)
        acc[...] = jnp.zeros(acc.shape, F32)
        line = (edge + start) // lanes
        qcode = jnp.concatenate(
            [codes_ref[pl.ds(line + j, 1), :] for j in range(BLOCK // lanes)], axis=1
        )

        def key_block(kb, c):
            k0 = pl.multiple_of(kb * BLOCK, BLOCK)
            kc = kcode[pl.ds(k0, BLOCK), :]
            kc = jnp.concatenate([kc] * (BLOCK // lanes), axis=1)
            bias[...] = jnp.where(kc == qcode, 0.0, FAR)
            kpart = kbuf[pl.ds(k0, BLOCK), :]
            for h in range(HEADS):
                s = dot(kpart, qz[h]) + bias[...]
                old = mbuf[h : h + 1, :]
                new = jnp.maximum(old, jnp.max(s, axis=0, keepdims=True))
                p = jnp.exp2((s - new).astype(BF16))
                grow = dot(vbuf[kb, h * VROWS : (h + 1) * VROWS, :], p)
                acc[h] = acc[h] * jnp.exp2(old - new) + grow
                mbuf[h : h + 1, :] = new
            return c

        lax.fori_loop(low // BLOCK, (high + BLOCK - 1) // BLOCK, key_block, 0)
        mixed = jnp.concatenate(
            [acc[h, 0:head, :] / acc[h, head : head + 1, :] for h in range(HEADS)], axis=0
        )
        attended = mixed.T.astype(BF16)
        after = (mine.astype(F32) + dot(attended, wo_ref[...])).astype(BF16)
        pre = dot(layer_norm(after, g2_ref[...]), up_ref[...])
        hidden = (0.5 * pre * (1.0 + lax.erf(pre * math.sqrt(0.5)))).astype(BF16)
        out_ref[pl.ds(start, BLOCK), :] = (after.astype(F32) + dot(hidden, down_ref[...])).astype(BF16)
        return carry

    lax.fori_loop(0, rows // BLOCK, query_block, 0)


def attention(ids, codes, mid, before, after, g1, wq, wk, wv, wo, g2, up, down):
    rows, channels = mid.shape
    total = rows + before.shape[0] + after.shape[0]
    vmem = pl.BlockSpec(memory_space=pltpu.VMEM)
    return pl.pallas_call(
        attn_kernel,
        out_shape=jax.ShapeDtypeStruct((rows, channels), BF16),
        in_specs=[pl.BlockSpec(memory_space=pltpu.SMEM)] + [vmem] * 12,
        out_specs=vmem,
        scratch_shapes=[
            pltpu.VMEM((total, channels), BF16),
            pltpu.VMEM((total // BLOCK, HEADS * VROWS, BLOCK), BF16),
            pltpu.VMEM((total, 128), F32),
            pltpu.VMEM((HEADS, channels, BLOCK), BF16),
            pltpu.VMEM((BLOCK, BLOCK), F32),
            pltpu.VMEM((HEADS, BLOCK), F32),
            pltpu.VMEM((HEADS, VROWS, BLOCK), F32),
        ],
        compiler_params=pltpu.CompilerParams(vmem_limit_bytes=48 * 2**20),
        name="attn",
    )(ids, codes, mid, before, after, g1, wq, wk, wv, wo, g2, up, down)


def decode(patch_codes):
    wide = patch_codes.astype(F32)
    return wide[0] * 64.0 + wide[1]


def body(
    feats, neighbours, send_rows, patch_ids, conv_weight, norm1_gain, query_weight,
    key_weight, value_weight, out_weight, norm2_gain, up_weight, down_weight,
):
    rows, channels = feats.shape
    peers = lax.axis_size("dev")
    slots = send_rows.shape[1] // peers
    shifted_ids = patch_ids + 1
    patch_codes = jnp.stack([shifted_ids // 64, shifted_ids % 64]).astype(F32).astype(BF16)
    both = ("region", "dev")
    before_codes = decode(shifted(patch_codes[:, rows - PMAX :], both, 1))
    after_codes = decode(shifted(patch_codes[:, :PMAX], both, -1))
    after_codes = jnp.where(after_codes == 0.0, 1e9, after_codes)
    codes = jnp.concatenate([before_codes, shifted_ids.astype(F32), after_codes]).reshape(-1, 128)

    outgoing = jnp.take(feats, send_rows[0], axis=0, mode="clip").reshape(peers, slots, channels)
    incoming = lax.all_to_all(outgoing, "dev", split_axis=0, concat_axis=0, tiled=True)
    after_conv = conv(feats, incoming.reshape(peers * slots, channels), neighbours, conv_weight)
    before = shifted(after_conv[rows - PMAX :], both, 1)
    after = shifted(after_conv[:PMAX], both, -1)
    return attention(
        patch_ids.reshape(1, rows), codes, after_conv, before, after,
        norm1_gain.reshape(1, channels), query_weight, key_weight, value_weight, out_weight,
        norm2_gain.reshape(1, channels), up_weight, down_weight,
    )


def solution(mesh):
    both = ("region", "dev")
    in_specs = (P(both, None), P(None, both), P(both, None), P(both)) + (P(),) * 9
    return jax.shard_map(
        body, mesh=mesh, in_specs=in_specs, out_specs=P(both, None), check_vma=False
    )
```

```python
import functools
import math

import jax
import jax.numpy as jnp
from jax import lax
from jax.experimental import pallas as pl
from jax.experimental.pallas import tpu as pltpu
from jax.sharding import PartitionSpec as P

HEADS = 8
PMAX = 1024
BLOCK = 256
CHUNK = 1024
CODE_ROWS = 16
LEAD = 8
VROWS = 32
FAR = -1e30
LIMIT = 80.0
F32 = jnp.float32
BF16 = jnp.bfloat16


def shifted(block, axis, distance):
    devices = range(lax.axis_size(axis))
    route = [(i - distance, i) for i in devices if i - distance in devices]
    return lax.ppermute(block, axis, route)


def layer_norm(inputs, norm_gain):
    inputs = inputs.astype(F32)
    center = inputs - jnp.mean(inputs, axis=-1, keepdims=True)
    spread = jnp.mean(center * center, axis=-1, keepdims=True)
    return (center * lax.rsqrt(spread + 1e-05) * norm_gain).astype(BF16)


def dot(a, b):
    return jnp.dot(a, b, preferred_element_type=F32)


def conv_kernel(nb_ref, feats_ref, inc_ref, ids_ref, w_ref, out_ref, first_ref, last_ref, tab, gath):
    step = pl.program_id(0)
    rows, channels = feats_ref.shape
    far = inc_ref.shape[0]
    taps, block, _ = gath.shape
    edge = first_ref.shape[0] - CODE_ROWS
    lines = edge // 128
    middle = taps // 2

    @pl.when(step == 0)
    def _():
        tab[0:LEAD, :] = jnp.zeros((LEAD, channels), F32)
        tab[LEAD : LEAD + rows, :] = feats_ref[...].astype(F32)
        tab[LEAD + rows : LEAD + rows + far, :] = inc_ref[...].astype(F32)

    def group(index, carry):
        base = pl.multiple_of(index * 8, 8)
        for tap in range(taps):
            if tap == middle:
                continue
            for j in range(8):
                row = nb_ref[tap * block + base + j]
                gath[tap, pl.ds(base + j, 1), :] = tab[pl.ds(row, 1), :]
        return carry

    lax.fori_loop(0, block // 8, group, 0)
    own = tab[pl.ds(pl.multiple_of(step * block + LEAD, 8), block), :]
    gath[middle] = own
    wide = jnp.concatenate([gath[tap].astype(BF16) for tap in range(taps)], axis=1)
    total = dot(wide, w_ref[...])
    result = (own + total).astype(BF16)
    out_ref[...] = result

    @pl.when(step < edge // block)
    def _():
        first_ref[pl.ds(pl.multiple_of(step * block, block), block), :] = result

    skipped = (rows - edge) // block

    @pl.when(step >= skipped)
    def _():
        last_ref[pl.ds(pl.multiple_of((step - skipped) * block, block), block), :] = result

    @pl.when(step == 0)
    def _():
        ids = ids_ref[...] + 1
        for ref, start in ((first_ref, 0), (last_ref, ids.shape[0] - lines)):
            part = ids[start : start + lines]
            high = jnp.right_shift(part, 6).astype(F32)
            low = jnp.bitwise_and(part, 63).astype(F32)
            ref[edge : edge + CODE_ROWS, :] = jnp.concatenate([high, low], axis=0).astype(BF16)


def conv(feats, incoming, flat, ids, conv_weight):
    rows, channels = feats.shape
    taps = conv_weight.shape[0]
    far = incoming.shape[0]
    block = min(BLOCK, rows)
    steps = rows // block
    vmem = pl.BlockSpec(memory_space=pltpu.VMEM)
    ends = jax.ShapeDtypeStruct((PMAX + CODE_ROWS, channels), BF16)
    return pl.pallas_call(
        conv_kernel,
        grid=(steps,),
        out_shape=(jax.ShapeDtypeStruct((rows, channels), BF16), ends, ends),
        in_specs=[
            pl.BlockSpec((flat.shape[0] // steps,), lambda i: (i,), memory_space=pltpu.SMEM),
            vmem, vmem, vmem, vmem,
        ],
        out_specs=(pl.BlockSpec((block, channels), lambda i: (i, 0)), vmem, vmem),
        scratch_shapes=[
            pltpu.VMEM((LEAD + rows + far, channels), F32),
            pltpu.VMEM((taps, block, channels), F32),
        ],
        compiler_params=pltpu.CompilerParams(vmem_limit_bytes=48 * 2**20),
        name="conv",
    )(flat, feats, incoming, ids, conv_weight.reshape(taps * channels, channels))


def flatten_neighbours(neighbours):
    taps, rows = neighbours.shape
    block = min(BLOCK, rows)
    steps = rows // block
    span = -(-taps * block // 1024) * 1024
    flat = (neighbours + LEAD).reshape(taps, steps, block).transpose(1, 0, 2).reshape(steps, taps * block)
    return jnp.pad(flat, ((0, 0), (0, span - taps * block))).reshape(-1)


def attn_kernel(
    ids_ref, lines_ref, mid_ref, before_ref, after_ref,
    g1_ref, wq_ref, wk_ref, wv_ref, wo_ref, g2_ref, up_ref, down_ref,
    out_ref, kbuf, vbuf, kcode, qz, bias, mbuf, acc, keep, kmax, codes_ref,
):
    rows, channels = mid_ref.shape
    head = channels // HEADS
    edge = before_ref.shape[0] - CODE_ROWS
    blocks = (rows + 2 * edge) // BLOCK
    lanes = codes_ref.shape[1]
    lines = edge // lanes
    inner = rows // lanes

    def decode(ref):
        wide = ref[edge : edge + CODE_ROWS, :].astype(F32)
        return wide[0:lines] * 64.0 + wide[lines : 2 * lines]

    codes_ref[0:lines, :] = decode(before_ref)
    codes_ref[lines : lines + inner, :] = (lines_ref[...] + 1).astype(F32)
    later = decode(after_ref)
    codes_ref[lines + inner : 2 * lines + inner, :] = jnp.where(later == 0.0, 1e9, later)
    g1 = g1_ref[...]

    kmax[...] = jnp.zeros(kmax.shape, F32)

    for slot in range(blocks):
        for h in range(HEADS):
            vbuf[slot, h * VROWS + head : (h + 1) * VROWS, :] = jnp.ones((VROWS - head, BLOCK), BF16)

    def side(ref, first, size):
        chunk = min(CHUNK, size)

        def one(i, carry):
            part = ref[pl.ds(pl.multiple_of(i * chunk, chunk), chunk), :]
            normed = layer_norm(part, g1)
            keys = dot(normed, wk_ref[...]).astype(BF16)
            base = pl.multiple_of(first * BLOCK + i * chunk, BLOCK)
            kbuf[pl.ds(base, chunk), :] = keys
            top = jnp.max(jnp.abs(keys.astype(F32)), axis=0, keepdims=True)
            kmax[0:1, :] = jnp.maximum(kmax[0:1, :], top)
            vt = dot(normed, wv_ref[...]).T.astype(BF16)
            for j in range(chunk // BLOCK):
                slot = first + i * (chunk // BLOCK) + j
                for h in range(HEADS):
                    vbuf[slot, h * VROWS : h * VROWS + head, :] = vt[
                        h * head : (h + 1) * head, j * BLOCK : (j + 1) * BLOCK
                    ]
            return carry
        lax.fori_loop(0, size // chunk, one, 0)

    side(before_ref, 0, edge)
    side(mid_ref, edge // BLOCK, rows)
    side(after_ref, (edge + rows) // BLOCK, edge)
    kmax[...] = jnp.broadcast_to(kmax[0:1, :], (128, channels)).T

    def code_column(i, carry):
        line = codes_ref[pl.ds(i, 1), :]
        kcode[pl.ds(pl.multiple_of(i * lanes, lanes), lanes), :] = jnp.broadcast_to(line, (lanes, lanes)).T
        return carry

    lax.fori_loop(0, codes_ref.shape[0], code_column, 0)
    all_codes = codes_ref[...]

    def query_block(i, carry):
        start = pl.multiple_of(i * BLOCK, BLOCK)
        mine = mid_ref[pl.ds(start, BLOCK), :]
        query = dot(layer_norm(mine, g1), wq_ref[...]) * (head ** (-0.5) * math.log2(math.e))
        qwide = query.T
        qt = qwide.astype(BF16)
        reach = jnp.concatenate([kmax[...]] * (BLOCK // 128), axis=1) * jnp.abs(qwide)
        bound = jnp.max(jnp.sum(reach.reshape(HEADS, head, BLOCK), axis=1))
        qz[...] = jnp.zeros(qz.shape, BF16)
        for h in range(HEADS):
            qz[h, h * head : (h + 1) * head, :] = qt[h * head : (h + 1) * head, :]
        first = ids_ref[0, start].astype(F32) + 1.0
        last = ids_ref[0, start + BLOCK - 1].astype(F32) + 1.0
        low = jnp.sum(jnp.where(all_codes < first, 1.0, 0.0)).astype(jnp.int32)
        high = jnp.sum(jnp.where(all_codes <= last, 1.0, 0.0)).astype(jnp.int32)
        acc[...] = jnp.zeros(acc.shape, F32)
        line = (edge + start) // lanes
        qcode = jnp.concatenate(
            [codes_ref[pl.ds(line + j, 1), :] for j in range(BLOCK // lanes)], axis=1
        )

        def key_block(kb, c):
            k0 = pl.multiple_of(kb * BLOCK, BLOCK)
            kc = kcode[pl.ds(k0, BLOCK), :]
            kc = jnp.concatenate([kc] * (BLOCK // lanes), axis=1)
            bias[...] = jnp.where(kc == qcode, 0.0, FAR)
            kpart = kbuf[pl.ds(k0, BLOCK), :]
            for h in range(HEADS):
                s = dot(kpart, qz[h]) + bias[...]
                old = mbuf[h : h + 1, :]
                new = jnp.maximum(old, jnp.max(s, axis=0, keepdims=True))
                p = jnp.exp2((s - new).astype(BF16))
                grow = dot(vbuf[kb, h * VROWS : (h + 1) * VROWS, :], p)
                acc[h] = acc[h] * jnp.exp2(old - new) + grow
                mbuf[h : h + 1, :] = new
            return c

        def key_block_bounded(kb, c):
            k0 = pl.multiple_of(kb * BLOCK, BLOCK)
            kc = kcode[pl.ds(k0, BLOCK), :]
            kc = jnp.concatenate([kc] * (BLOCK // lanes), axis=1)
            keep[...] = jnp.where(kc == qcode, 1.0, 0.0).astype(BF16)
            kpart = kbuf[pl.ds(k0, BLOCK), :]
            wide = jnp.exp2(dot(kpart, jnp.concatenate([qz[h] for h in range(HEADS)], axis=1)))
            parts = [wide[:, h * BLOCK : (h + 1) * BLOCK].astype(BF16) * keep[...] for h in range(HEADS)]
            for h in range(HEADS):
                acc[h] = acc[h] + dot(vbuf[kb, h * VROWS : (h + 1) * VROWS, :], parts[h])
            return c

        kb_low, kb_high = low // BLOCK, (high + BLOCK - 1) // BLOCK

        @pl.when(bound < LIMIT)
        def _():
            lax.fori_loop(kb_low, kb_high, key_block_bounded, 0)

        @pl.when(jnp.logical_not(bound < LIMIT))
        def _():
            mbuf[...] = jnp.full(mbuf.shape, FAR, F32)
            lax.fori_loop(kb_low, kb_high, key_block, 0)

        mixed = jnp.concatenate(
            [acc[h, 0:head, :] / acc[h, head : head + 1, :] for h in range(HEADS)], axis=0
        )
        attended = mixed.T.astype(BF16)
        after = (mine.astype(F32) + dot(attended, wo_ref[...])).astype(BF16)
        pre = dot(layer_norm(after, g2_ref[...]), up_ref[...])
        hidden = (0.5 * pre * (1.0 + lax.erf(pre * math.sqrt(0.5)))).astype(BF16)
        out_ref[pl.ds(start, BLOCK), :] = (after.astype(F32) + dot(hidden, down_ref[...])).astype(BF16)
        return carry

    lax.fori_loop(0, rows // BLOCK, query_block, 0)


def attention(ids, lines, mid, before, after, g1, wq, wk, wv, wo, g2, up, down):
    rows, channels = mid.shape
    total = rows + 2 * PMAX
    vmem = pl.BlockSpec(memory_space=pltpu.VMEM)
    return pl.pallas_call(
        attn_kernel,
        out_shape=jax.ShapeDtypeStruct((rows, channels), BF16),
        in_specs=[pl.BlockSpec(memory_space=pltpu.SMEM)] + [vmem] * 12,
        out_specs=vmem,
        scratch_shapes=[
            pltpu.VMEM((total, channels), BF16),
            pltpu.VMEM((total // BLOCK, HEADS * VROWS, BLOCK), BF16),
            pltpu.VMEM((total, 128), F32),
            pltpu.VMEM((HEADS, channels, BLOCK), BF16),
            pltpu.VMEM((BLOCK, BLOCK), F32),
            pltpu.VMEM((HEADS, BLOCK), F32),
            pltpu.VMEM((HEADS, VROWS, BLOCK), F32),
            pltpu.VMEM((BLOCK, BLOCK), BF16),
            pltpu.VMEM((channels, 128), F32),
            pltpu.VMEM((total // 128, 128), F32),
        ],
        compiler_params=pltpu.CompilerParams(vmem_limit_bytes=48 * 2**20),
        name="attn",
    )(ids, lines, mid, before, after, g1, wq, wk, wv, wo, g2, up, down)


def body(
    feats, neighbours, send_rows, patch_ids, conv_weight, norm1_gain, query_weight,
    key_weight, value_weight, out_weight, norm2_gain, up_weight, down_weight,
):
    rows, channels = feats.shape
    peers = lax.axis_size("dev")
    slots = send_rows.shape[1] // peers
    both = ("region", "dev")
    lines = patch_ids.reshape(rows // 128, 128)
    flat = flatten_neighbours(neighbours)
    outgoing = jnp.take(feats, send_rows[0], axis=0, mode="clip").reshape(peers, slots, channels)
    incoming = lax.all_to_all(outgoing, "dev", split_axis=0, concat_axis=0, tiled=True)
    after_conv, first, last = conv(
        feats, incoming.reshape(peers * slots, channels), flat, lines, conv_weight
    )
    before = shifted(last, both, 1)
    after = shifted(first, both, -1)
    return attention(
        patch_ids.reshape(1, rows), lines, after_conv, before, after,
        norm1_gain.reshape(1, channels), query_weight, key_weight, value_weight, out_weight,
        norm2_gain.reshape(1, channels), up_weight, down_weight,
    )


def solution(mesh):
    both = ("region", "dev")
    in_specs = (P(both, None), P(None, both), P(both, None), P(both)) + (P(),) * 9
    return jax.shard_map(
        body, mesh=mesh, in_specs=in_specs, out_specs=P(both, None), check_vma=False
    )
```

```python
import functools
import math

import jax
import jax.numpy as jnp
from jax import lax
from jax.experimental import pallas as pl
from jax.experimental.pallas import tpu as pltpu
from jax.sharding import PartitionSpec as P

HEADS = 8
PMAX = 1024
BLOCK = 256
CHUNK = 1024
CODE_ROWS = 16
LEAD = 8
VROWS = 32
FAR = -1e30
LIMIT = 80.0
F32 = jnp.float32
BF16 = jnp.bfloat16


MESH = pl.DeviceIdType.MESH


def exchange_kernel(rows_ref, feats_ref, out_ref, tab, picked, outgoing, send_sems, recv_sems):
    peers, slots, channels = out_ref.shape
    region, me = lax.axis_index("region"), lax.axis_index("dev")
    barrier = pltpu.get_barrier_semaphore()
    for offset in range(1, peers):
        peer = lax.rem(me + offset, peers)
        pl.semaphore_signal(barrier, inc=1, device_id=(region, peer), device_id_type=MESH)
    tab[...] = feats_ref[...].astype(F32)

    def group(index, carry):
        base = pl.multiple_of(index * 8, 8)
        for j in range(8):
            picked[pl.ds(base + j, 1), :] = tab[pl.ds(rows_ref[base + j], 1), :]
        return carry

    lax.fori_loop(0, peers * slots // 8, group, 0)
    outgoing[...] = picked[...].astype(BF16).reshape(peers, slots, channels)
    pl.semaphore_wait(barrier, peers - 1)

    def copy(peer, source):
        return pltpu.make_async_remote_copy(
            src_ref=outgoing.at[peer],
            dst_ref=out_ref.at[source],
            send_sem=send_sems.at[peer],
            recv_sem=recv_sems.at[source],
            device_id=(region, peer),
            device_id_type=MESH,
        )

    for offset in range(1, peers):
        copy(lax.rem(me + offset, peers), me).start()
    out_ref[pl.ds(me, 1)] = outgoing[pl.ds(me, 1)]
    for offset in range(1, peers):
        peer = lax.rem(me + offset, peers)
        copy(peer, me).wait_send()
        copy(peer, peer).wait_recv()


def exchange(send_rows, feats, peers):
    rows, channels = feats.shape
    slots = send_rows.shape[0] // peers
    vmem = pl.BlockSpec(memory_space=pltpu.VMEM)
    return pl.pallas_call(
        exchange_kernel,
        out_shape=jax.ShapeDtypeStruct((peers, slots, channels), BF16),
        in_specs=[pl.BlockSpec(memory_space=pltpu.SMEM), vmem],
        out_specs=vmem,
        scratch_shapes=[
            pltpu.VMEM((rows, channels), F32),
            pltpu.VMEM((peers * slots, channels), F32),
            pltpu.VMEM((peers, slots, channels), BF16),
            pltpu.SemaphoreType.DMA((peers,)),
            pltpu.SemaphoreType.DMA((peers,)),
        ],
        compiler_params=pltpu.CompilerParams(
            collective_id=1, has_side_effects=True, vmem_limit_bytes=24 * 2**20
        ),
        name="exchange",
    )(send_rows, feats)


def edges_kernel(first_ref, last_ref, before_ref, after_ref, send_sems, recv_sems):
    width = lax.axis_size("dev")
    total = lax.axis_size("region") * width
    me = lax.axis_index("region") * width + lax.axis_index("dev")
    barrier = pltpu.get_barrier_semaphore()
    has_left, has_right = me > 0, me < total - 1

    def place(index):
        return (index // width, lax.rem(index, width))

    def to_right():
        return pltpu.make_async_remote_copy(
            src_ref=last_ref, dst_ref=before_ref, send_sem=send_sems.at[0], recv_sem=recv_sems.at[0],
            device_id=place(me + 1), device_id_type=MESH,
        )

    def to_left():
        return pltpu.make_async_remote_copy(
            src_ref=first_ref, dst_ref=after_ref, send_sem=send_sems.at[1], recv_sem=recv_sems.at[1],
            device_id=place(me - 1), device_id_type=MESH,
        )

    @pl.when(has_left)
    def _():
        pl.semaphore_signal(barrier, inc=1, device_id=place(me - 1), device_id_type=MESH)

    @pl.when(has_right)
    def _():
        pl.semaphore_signal(barrier, inc=1, device_id=place(me + 1), device_id_type=MESH)

    pl.semaphore_wait(barrier, jnp.minimum(me, 1) + jnp.minimum(total - 1 - me, 1))

    @pl.when(has_right)
    def _():
        to_right().start()

    @pl.when(has_left)
    def _():
        to_left().start()

    @pl.when(me == 0)
    def _():
        before_ref[...] = jnp.zeros(before_ref.shape, BF16)

    @pl.when(me == total - 1)
    def _():
        after_ref[...] = jnp.zeros(after_ref.shape, BF16)

    @pl.when(has_right)
    def _():
        to_right().wait_send()
        to_left().wait_recv()

    @pl.when(has_left)
    def _():
        to_left().wait_send()
        to_right().wait_recv()


def edges(first, last):
    vmem = pl.BlockSpec(memory_space=pltpu.VMEM)
    return pl.pallas_call(
        edges_kernel,
        out_shape=(jax.ShapeDtypeStruct(last.shape, BF16), jax.ShapeDtypeStruct(first.shape, BF16)),
        in_specs=[vmem, vmem],
        out_specs=(vmem, vmem),
        scratch_shapes=[pltpu.SemaphoreType.DMA((2,)), pltpu.SemaphoreType.DMA((2,))],
        compiler_params=pltpu.CompilerParams(collective_id=2, has_side_effects=True),
        name="edges",
    )(first, last)


def layer_norm(inputs, norm_gain):
    inputs = inputs.astype(F32)
    center = inputs - jnp.mean(inputs, axis=-1, keepdims=True)
    spread = jnp.mean(center * center, axis=-1, keepdims=True)
    return (center * lax.rsqrt(spread + 1e-05) * norm_gain).astype(BF16)


def dot(a, b):
    return jnp.dot(a, b, preferred_element_type=F32)


def conv_kernel(nb_ref, feats_ref, inc_ref, ids_ref, w_ref, out_ref, first_ref, last_ref, tab, gath):
    step = pl.program_id(0)
    rows, channels = feats_ref.shape
    far = inc_ref.shape[0]
    taps, block, _ = gath.shape
    edge = first_ref.shape[0] - CODE_ROWS
    lines = edge // 128
    middle = taps // 2

    @pl.when(step == 0)
    def _():
        tab[0:LEAD, :] = jnp.zeros((LEAD, channels), F32)
        tab[LEAD : LEAD + rows, :] = feats_ref[...].astype(F32)
        tab[LEAD + rows : LEAD + rows + far, :] = inc_ref[...].astype(F32)

    def group(index, carry):
        base = pl.multiple_of(index * 8, 8)
        for tap in range(taps):
            if tap == middle:
                continue
            for j in range(8):
                row = nb_ref[tap * block + base + j]
                gath[tap, pl.ds(base + j, 1), :] = tab[pl.ds(row, 1), :]
        return carry

    lax.fori_loop(0, block // 8, group, 0)
    own = tab[pl.ds(pl.multiple_of(step * block + LEAD, 8), block), :]
    gath[middle] = own
    wide = jnp.concatenate([gath[tap].astype(BF16) for tap in range(taps)], axis=1)
    total = dot(wide, w_ref[...])
    result = (own + total).astype(BF16)
    out_ref[...] = result

    @pl.when(step < edge // block)
    def _():
        first_ref[pl.ds(pl.multiple_of(step * block, block), block), :] = result

    skipped = (rows - edge) // block

    @pl.when(step >= skipped)
    def _():
        last_ref[pl.ds(pl.multiple_of((step - skipped) * block, block), block), :] = result

    @pl.when(step == 0)
    def _():
        ids = ids_ref[...] + 1
        for ref, start in ((first_ref, 0), (last_ref, ids.shape[0] - lines)):
            part = ids[start : start + lines]
            high = jnp.right_shift(part, 6).astype(F32)
            low = jnp.bitwise_and(part, 63).astype(F32)
            ref[edge : edge + CODE_ROWS, :] = jnp.concatenate([high, low], axis=0).astype(BF16)


def conv(feats, incoming, flat, ids, conv_weight):
    rows, channels = feats.shape
    taps = conv_weight.shape[0]
    far = incoming.shape[0]
    block = min(BLOCK, rows)
    steps = rows // block
    vmem = pl.BlockSpec(memory_space=pltpu.VMEM)
    ends = jax.ShapeDtypeStruct((PMAX + CODE_ROWS, channels), BF16)
    return pl.pallas_call(
        conv_kernel,
        grid=(steps,),
        out_shape=(jax.ShapeDtypeStruct((rows, channels), BF16), ends, ends),
        in_specs=[
            pl.BlockSpec((flat.shape[0] // steps,), lambda i: (i,), memory_space=pltpu.SMEM),
            vmem, vmem, vmem, vmem,
        ],
        out_specs=(pl.BlockSpec((block, channels), lambda i: (i, 0)), vmem, vmem),
        scratch_shapes=[
            pltpu.VMEM((LEAD + rows + far, channels), F32),
            pltpu.VMEM((taps, block, channels), F32),
        ],
        compiler_params=pltpu.CompilerParams(vmem_limit_bytes=48 * 2**20),
        name="conv",
    )(flat, feats, incoming, ids, conv_weight.reshape(taps * channels, channels))


def flatten_neighbours(neighbours):
    taps, rows = neighbours.shape
    block = min(BLOCK, rows)
    steps = rows // block
    span = -(-taps * block // 1024) * 1024
    flat = (neighbours + LEAD).reshape(taps, steps, block).transpose(1, 0, 2).reshape(steps, taps * block)
    return jnp.pad(flat, ((0, 0), (0, span - taps * block))).reshape(-1)


def attn_kernel(
    ids_ref, lines_ref, mid_ref, before_ref, after_ref,
    g1_ref, wq_ref, wk_ref, wv_ref, wo_ref, g2_ref, up_ref, down_ref,
    out_ref, kbuf, vbuf, kcode, qz, bias, mbuf, acc, keep, kmax, codes_ref,
):
    rows, channels = mid_ref.shape
    head = channels // HEADS
    edge = before_ref.shape[0] - CODE_ROWS
    blocks = (rows + 2 * edge) // BLOCK
    lanes = codes_ref.shape[1]
    lines = edge // lanes
    inner = rows // lanes

    def decode(ref):
        wide = ref[edge : edge + CODE_ROWS, :].astype(F32)
        return wide[0:lines] * 64.0 + wide[lines : 2 * lines]

    codes_ref[0:lines, :] = decode(before_ref)
    codes_ref[lines : lines + inner, :] = (lines_ref[...] + 1).astype(F32)
    later = decode(after_ref)
    codes_ref[lines + inner : 2 * lines + inner, :] = jnp.where(later == 0.0, 1e9, later)
    g1 = g1_ref[...]

    kmax[...] = jnp.zeros(kmax.shape, F32)

    for slot in range(blocks):
        for h in range(HEADS):
            vbuf[slot, h * VROWS + head : (h + 1) * VROWS, :] = jnp.ones((VROWS - head, BLOCK), BF16)

    def side(ref, first, size):
        chunk = min(CHUNK, size)

        def one(i, carry):
            part = ref[pl.ds(pl.multiple_of(i * chunk, chunk), chunk), :]
            normed = layer_norm(part, g1)
            keys = dot(normed, wk_ref[...]).astype(BF16)
            base = pl.multiple_of(first * BLOCK + i * chunk, BLOCK)
            kbuf[pl.ds(base, chunk), :] = keys
            top = jnp.max(jnp.abs(keys.astype(F32)), axis=0, keepdims=True)
            kmax[0:1, :] = jnp.maximum(kmax[0:1, :], top)
            vt = dot(normed, wv_ref[...]).T.astype(BF16)
            for j in range(chunk // BLOCK):
                slot = first + i * (chunk // BLOCK) + j
                for h in range(HEADS):
                    vbuf[slot, h * VROWS : h * VROWS + head, :] = vt[
                        h * head : (h + 1) * head, j * BLOCK : (j + 1) * BLOCK
                    ]
            return carry
        lax.fori_loop(0, size // chunk, one, 0)

    side(before_ref, 0, edge)
    side(mid_ref, edge // BLOCK, rows)
    side(after_ref, (edge + rows) // BLOCK, edge)
    kmax[...] = jnp.broadcast_to(kmax[0:1, :], (128, channels)).T

    def code_column(i, carry):
        line = codes_ref[pl.ds(i, 1), :]
        kcode[pl.ds(pl.multiple_of(i * lanes, lanes), lanes), :] = jnp.broadcast_to(line, (lanes, lanes)).T
        return carry

    lax.fori_loop(0, codes_ref.shape[0], code_column, 0)
    all_codes = codes_ref[...]

    def query_block(i, carry):
        start = pl.multiple_of(i * BLOCK, BLOCK)
        mine = mid_ref[pl.ds(start, BLOCK), :]
        query = dot(layer_norm(mine, g1), wq_ref[...]) * (head ** (-0.5) * math.log2(math.e))
        qwide = query.T
        qt = qwide.astype(BF16)
        reach = jnp.concatenate([kmax[...]] * (BLOCK // 128), axis=1) * jnp.abs(qwide)
        bound = jnp.max(jnp.sum(reach.reshape(HEADS, head, BLOCK), axis=1))
        qz[...] = jnp.zeros(qz.shape, BF16)
        for h in range(HEADS):
            qz[h, h * head : (h + 1) * head, :] = qt[h * head : (h + 1) * head, :]
        first = ids_ref[0, start].astype(F32) + 1.0
        last = ids_ref[0, start + BLOCK - 1].astype(F32) + 1.0
        low = jnp.sum(jnp.where(all_codes < first, 1.0, 0.0)).astype(jnp.int32)
        high = jnp.sum(jnp.where(all_codes <= last, 1.0, 0.0)).astype(jnp.int32)
        acc[...] = jnp.zeros(acc.shape, F32)
        line = (edge + start) // lanes
        qcode = jnp.concatenate(
            [codes_ref[pl.ds(line + j, 1), :] for j in range(BLOCK // lanes)], axis=1
        )

        def key_block(kb, c):
            k0 = pl.multiple_of(kb * BLOCK, BLOCK)
            kc = kcode[pl.ds(k0, BLOCK), :]
            kc = jnp.concatenate([kc] * (BLOCK // lanes), axis=1)
            bias[...] = jnp.where(kc == qcode, 0.0, FAR)
            kpart = kbuf[pl.ds(k0, BLOCK), :]
            for h in range(HEADS):
                s = dot(kpart, qz[h]) + bias[...]
                old = mbuf[h : h + 1, :]
                new = jnp.maximum(old, jnp.max(s, axis=0, keepdims=True))
                p = jnp.exp2((s - new).astype(BF16))
                grow = dot(vbuf[kb, h * VROWS : (h + 1) * VROWS, :], p)
                acc[h] = acc[h] * jnp.exp2(old - new) + grow
                mbuf[h : h + 1, :] = new
            return c

        def key_block_bounded(kb, c):
            k0 = pl.multiple_of(kb * BLOCK, BLOCK)
            kc = kcode[pl.ds(k0, BLOCK), :]
            kc = jnp.concatenate([kc] * (BLOCK // lanes), axis=1)
            keep[...] = jnp.where(kc == qcode, 1.0, 0.0).astype(BF16)
            kpart = kbuf[pl.ds(k0, BLOCK), :]
            wide = jnp.exp2(dot(kpart, jnp.concatenate([qz[h] for h in range(HEADS)], axis=1)))
            parts = [wide[:, h * BLOCK : (h + 1) * BLOCK].astype(BF16) * keep[...] for h in range(HEADS)]
            for h in range(HEADS):
                acc[h] = acc[h] + dot(vbuf[kb, h * VROWS : (h + 1) * VROWS, :], parts[h])
            return c

        kb_low, kb_high = low // BLOCK, (high + BLOCK - 1) // BLOCK

        @pl.when(bound < LIMIT)
        def _():
            lax.fori_loop(kb_low, kb_high, key_block_bounded, 0)

        @pl.when(jnp.logical_not(bound < LIMIT))
        def _():
            mbuf[...] = jnp.full(mbuf.shape, FAR, F32)
            lax.fori_loop(kb_low, kb_high, key_block, 0)

        mixed = jnp.concatenate(
            [acc[h, 0:head, :] / acc[h, head : head + 1, :] for h in range(HEADS)], axis=0
        )
        attended = mixed.T.astype(BF16)
        after = (mine.astype(F32) + dot(attended, wo_ref[...])).astype(BF16)
        pre = dot(layer_norm(after, g2_ref[...]), up_ref[...])
        hidden = (0.5 * pre * (1.0 + lax.erf(pre * math.sqrt(0.5)))).astype(BF16)
        out_ref[pl.ds(start, BLOCK), :] = (after.astype(F32) + dot(hidden, down_ref[...])).astype(BF16)
        return carry

    lax.fori_loop(0, rows // BLOCK, query_block, 0)


def attention(ids, lines, mid, before, after, g1, wq, wk, wv, wo, g2, up, down):
    rows, channels = mid.shape
    total = rows + 2 * PMAX
    vmem = pl.BlockSpec(memory_space=pltpu.VMEM)
    return pl.pallas_call(
        attn_kernel,
        out_shape=jax.ShapeDtypeStruct((rows, channels), BF16),
        in_specs=[pl.BlockSpec(memory_space=pltpu.SMEM)] + [vmem] * 12,
        out_specs=vmem,
        scratch_shapes=[
            pltpu.VMEM((total, channels), BF16),
            pltpu.VMEM((total // BLOCK, HEADS * VROWS, BLOCK), BF16),
            pltpu.VMEM((total, 128), F32),
            pltpu.VMEM((HEADS, channels, BLOCK), BF16),
            pltpu.VMEM((BLOCK, BLOCK), F32),
            pltpu.VMEM((HEADS, BLOCK), F32),
            pltpu.VMEM((HEADS, VROWS, BLOCK), F32),
            pltpu.VMEM((BLOCK, BLOCK), BF16),
            pltpu.VMEM((channels, 128), F32),
            pltpu.VMEM((total // 128, 128), F32),
        ],
        compiler_params=pltpu.CompilerParams(vmem_limit_bytes=48 * 2**20),
        name="attn",
    )(ids, lines, mid, before, after, g1, wq, wk, wv, wo, g2, up, down)


def body(
    feats, neighbours, send_rows, patch_ids, conv_weight, norm1_gain, query_weight,
    key_weight, value_weight, out_weight, norm2_gain, up_weight, down_weight,
):
    rows, channels = feats.shape
    peers = lax.axis_size("dev")
    slots = send_rows.shape[1] // peers
    lines = patch_ids.reshape(rows // 128, 128)
    flat = flatten_neighbours(neighbours)
    incoming = exchange(send_rows.reshape(peers * slots), feats, peers)
    after_conv, first, last = conv(
        feats, incoming.reshape(peers * slots, channels), flat, lines, conv_weight
    )
    before, after = edges(first, last)
    return attention(
        patch_ids.reshape(1, rows), lines, after_conv, before, after,
        norm1_gain.reshape(1, channels), query_weight, key_weight, value_weight, out_weight,
        norm2_gain.reshape(1, channels), up_weight, down_weight,
    )


def solution(mesh):
    both = ("region", "dev")
    in_specs = (P(both, None), P(None, both), P(both, None), P(both)) + (P(),) * 9
    return jax.shard_map(
        body, mesh=mesh, in_specs=in_specs, out_specs=P(both, None), check_vma=False
    )
```

```python
import functools
import math

import jax
import jax.numpy as jnp
from jax import lax
from jax.experimental import pallas as pl
from jax.experimental.pallas import tpu as pltpu
from jax.sharding import PartitionSpec as P

HEADS = 8
PMAX = 1024
BLOCK = 256
CHUNK = 1024
CODE_ROWS = 16
LEAD = 8
VROWS = 32
FAR = -1e30
LIMIT = 80.0
F32 = jnp.float32
BF16 = jnp.bfloat16


MESH = pl.DeviceIdType.MESH


def exchange_kernel(rows_ref, feats_ref, out_ref, tab, picked, outgoing, send_sems, recv_sems):
    peers, slots, channels = out_ref.shape
    region, me = lax.axis_index("region"), lax.axis_index("dev")
    barrier = pltpu.get_barrier_semaphore()
    for offset in range(1, peers):
        peer = lax.rem(me + offset, peers)
        pl.semaphore_signal(barrier, inc=1, device_id=(region, peer), device_id_type=MESH)
    tab[...] = feats_ref[...].astype(F32)

    def group(index, carry):
        base = pl.multiple_of(index * 8, 8)
        for j in range(8):
            picked[pl.ds(base + j, 1), :] = tab[pl.ds(rows_ref[base + j], 1), :]
        return carry

    lax.fori_loop(0, peers * slots // 8, group, 0)
    outgoing[...] = picked[...].astype(BF16).reshape(peers, slots, channels)
    pl.semaphore_wait(barrier, peers - 1)

    def copy(peer, source):
        return pltpu.make_async_remote_copy(
            src_ref=outgoing.at[peer],
            dst_ref=out_ref.at[source],
            send_sem=send_sems.at[peer],
            recv_sem=recv_sems.at[source],
            device_id=(region, peer),
            device_id_type=MESH,
        )

    for offset in range(1, peers):
        copy(lax.rem(me + offset, peers), me).start()
    out_ref[pl.ds(me, 1)] = outgoing[pl.ds(me, 1)]
    for offset in range(1, peers):
        peer = lax.rem(me + offset, peers)
        copy(peer, me).wait_send()
        copy(peer, peer).wait_recv()


def exchange(send_rows, feats, peers):
    rows, channels = feats.shape
    slots = send_rows.shape[0] // peers
    vmem = pl.BlockSpec(memory_space=pltpu.VMEM)
    return pl.pallas_call(
        exchange_kernel,
        out_shape=jax.ShapeDtypeStruct((peers, slots, channels), BF16),
        in_specs=[pl.BlockSpec(memory_space=pltpu.SMEM), vmem],
        out_specs=vmem,
        scratch_shapes=[
            pltpu.VMEM((rows, channels), F32),
            pltpu.VMEM((peers * slots, channels), F32),
            pltpu.VMEM((peers, slots, channels), BF16),
            pltpu.SemaphoreType.DMA((peers,)),
            pltpu.SemaphoreType.DMA((peers,)),
        ],
        compiler_params=pltpu.CompilerParams(
            collective_id=1, has_side_effects=True, vmem_limit_bytes=24 * 2**20
        ),
        name="exchange",
    )(send_rows, feats)


def shifted(block, axis, distance):
    devices = range(lax.axis_size(axis))
    route = [(i - distance, i) for i in devices if i - distance in devices]
    return lax.ppermute(block, axis, route)


def layer_norm(inputs, norm_gain):
    inputs = inputs.astype(F32)
    center = inputs - jnp.mean(inputs, axis=-1, keepdims=True)
    spread = jnp.mean(center * center, axis=-1, keepdims=True)
    return (center * lax.rsqrt(spread + 1e-05) * norm_gain).astype(BF16)


def dot(a, b):
    return jnp.dot(a, b, preferred_element_type=F32)


def conv_kernel(first, nb_ref, feats_ref, inc_ref, ids_ref, w_ref, out_ref, tab, gath):
    step = pl.program_id(0)
    rows, channels = feats_ref.shape
    far = inc_ref.shape[0]
    taps, block, _ = gath.shape
    edge = out_ref.shape[0] - CODE_ROWS
    lines = edge // 128
    middle = taps // 2

    @pl.when(step == 0)
    def _():
        tab[0:LEAD, :] = jnp.zeros((LEAD, channels), F32)
        tab[LEAD : LEAD + rows, :] = feats_ref[...].astype(F32)
        tab[LEAD + rows : LEAD + rows + far, :] = inc_ref[...].astype(F32)

    def group(index, carry):
        base = pl.multiple_of(index * 8, 8)
        for tap in range(taps):
            if tap == middle:
                continue
            for j in range(8):
                row = nb_ref[tap * block + base + j]
                gath[tap, pl.ds(base + j, 1), :] = tab[pl.ds(row, 1), :]
        return carry

    lax.fori_loop(0, block // 8, group, 0)
    own = tab[pl.ds(pl.multiple_of(step * block + first + LEAD, 8), block), :]
    gath[middle] = own
    wide = jnp.concatenate([gath[tap].astype(BF16) for tap in range(taps)], axis=1)
    total = dot(wide, w_ref[...])
    out_ref[pl.ds(pl.multiple_of(step * block, block), block), :] = (own + total).astype(BF16)

    @pl.when(step == 0)
    def _():
        ids = ids_ref[first // 128 : first // 128 + lines, :] + 1
        high = jnp.right_shift(ids, 6).astype(F32)
        low = jnp.bitwise_and(ids, 63).astype(F32)
        out_ref[edge : edge + CODE_ROWS, :] = jnp.concatenate([high, low], axis=0).astype(BF16)


def conv(feats, incoming, flat, ids, conv_weight, first):
    rows, channels = feats.shape
    taps = conv_weight.shape[0]
    far = incoming.shape[0]
    block = min(BLOCK, rows)
    skip = first // block
    vmem = pl.BlockSpec(memory_space=pltpu.VMEM)
    ends = jax.ShapeDtypeStruct((PMAX + CODE_ROWS, channels), BF16)
    return pl.pallas_call(
        functools.partial(conv_kernel, first),
        grid=(PMAX // block,),
        out_shape=ends,
        in_specs=[
            pl.BlockSpec((flat.shape[0] // (rows // block),), lambda i: (i + skip,), memory_space=pltpu.SMEM),
            vmem, vmem, vmem, vmem,
        ],
        out_specs=vmem,
        scratch_shapes=[
            pltpu.VMEM((LEAD + rows + far, channels), F32),
            pltpu.VMEM((taps, block, channels), F32),
        ],
        compiler_params=pltpu.CompilerParams(vmem_limit_bytes=48 * 2**20),
        cost_estimate=pl.CostEstimate(flops=2 * 10**10, bytes_accessed=2 * 10**6, transcendentals=0),
        name="conv",
    )(flat, feats, incoming, ids, conv_weight.reshape(taps * channels, channels))


def flatten_neighbours(neighbours):
    taps, rows = neighbours.shape
    block = min(BLOCK, rows)
    steps = rows // block
    span = -(-taps * block // 1024) * 1024
    flat = (neighbours + LEAD).reshape(taps, steps, block).transpose(1, 0, 2).reshape(steps, taps * block)
    return jnp.pad(flat, ((0, 0), (0, span - taps * block))).reshape(-1)


def attn_kernel(
    ids_ref, lines_ref, first_ref, last_ref, before_ref, after_ref,
    g1_ref, wq_ref, wk_ref, wv_ref, wo_ref, g2_ref, up_ref, down_ref,
    out_ref, kbuf, vbuf, kcode, qz, bias, mbuf, acc, keep, kmax, codes_ref, mid_ref,
):
    rows, channels = mid_ref.shape
    head = channels // HEADS
    edge = before_ref.shape[0] - CODE_ROWS
    blocks = (rows + 2 * edge) // BLOCK
    lanes = codes_ref.shape[1]
    lines = edge // lanes
    mid_ref[0:edge, :] = first_ref[0:edge, :]
    mid_ref[rows - edge : rows, :] = last_ref[0:edge, :]
    inner = rows // lanes

    def decode(ref):
        wide = ref[edge : edge + CODE_ROWS, :].astype(F32)
        return wide[0:lines] * 64.0 + wide[lines : 2 * lines]

    codes_ref[0:lines, :] = decode(before_ref)
    codes_ref[lines : lines + inner, :] = (lines_ref[...] + 1).astype(F32)
    later = decode(after_ref)
    codes_ref[lines + inner : 2 * lines + inner, :] = jnp.where(later == 0.0, 1e9, later)
    g1 = g1_ref[...]

    kmax[...] = jnp.zeros(kmax.shape, F32)

    for slot in range(blocks):
        for h in range(HEADS):
            vbuf[slot, h * VROWS + head : (h + 1) * VROWS, :] = jnp.ones((VROWS - head, BLOCK), BF16)

    def side(ref, first, size):
        chunk = min(CHUNK, size)

        def one(i, carry):
            part = ref[pl.ds(pl.multiple_of(i * chunk, chunk), chunk), :]
            normed = layer_norm(part, g1)
            keys = dot(normed, wk_ref[...]).astype(BF16)
            base = pl.multiple_of(first * BLOCK + i * chunk, BLOCK)
            kbuf[pl.ds(base, chunk), :] = keys
            top = jnp.max(jnp.abs(keys.astype(F32)), axis=0, keepdims=True)
            kmax[0:1, :] = jnp.maximum(kmax[0:1, :], top)
            vt = dot(normed, wv_ref[...]).T.astype(BF16)
            for j in range(chunk // BLOCK):
                slot = first + i * (chunk // BLOCK) + j
                for h in range(HEADS):
                    vbuf[slot, h * VROWS : h * VROWS + head, :] = vt[
                        h * head : (h + 1) * head, j * BLOCK : (j + 1) * BLOCK
                    ]
            return carry
        lax.fori_loop(0, size // chunk, one, 0)

    side(before_ref, 0, edge)
    side(mid_ref, edge // BLOCK, rows)
    side(after_ref, (edge + rows) // BLOCK, edge)
    kmax[...] = jnp.broadcast_to(kmax[0:1, :], (128, channels)).T

    def code_column(i, carry):
        line = codes_ref[pl.ds(i, 1), :]
        kcode[pl.ds(pl.multiple_of(i * lanes, lanes), lanes), :] = jnp.broadcast_to(line, (lanes, lanes)).T
        return carry

    lax.fori_loop(0, codes_ref.shape[0], code_column, 0)
    all_codes = codes_ref[...]

    def query_block(i, carry):
        start = pl.multiple_of(i * BLOCK, BLOCK)
        mine = mid_ref[pl.ds(start, BLOCK), :]
        query = dot(layer_norm(mine, g1), wq_ref[...]) * (head ** (-0.5) * math.log2(math.e))
        qwide = query.T
        qt = qwide.astype(BF16)
        reach = jnp.concatenate([kmax[...]] * (BLOCK // 128), axis=1) * jnp.abs(qwide)
        bound = jnp.max(jnp.sum(reach.reshape(HEADS, head, BLOCK), axis=1))
        qz[...] = jnp.zeros(qz.shape, BF16)
        for h in range(HEADS):
            qz[h, h * head : (h + 1) * head, :] = qt[h * head : (h + 1) * head, :]
        first = ids_ref[0, start].astype(F32) + 1.0
        last = ids_ref[0, start + BLOCK - 1].astype(F32) + 1.0
        low = jnp.sum(jnp.where(all_codes < first, 1.0, 0.0)).astype(jnp.int32)
        high = jnp.sum(jnp.where(all_codes <= last, 1.0, 0.0)).astype(jnp.int32)
        acc[...] = jnp.zeros(acc.shape, F32)
        line = (edge + start) // lanes
        qcode = jnp.concatenate(
            [codes_ref[pl.ds(line + j, 1), :] for j in range(BLOCK // lanes)], axis=1
        )

        def key_block(kb, c):
            k0 = pl.multiple_of(kb * BLOCK, BLOCK)
            kc = kcode[pl.ds(k0, BLOCK), :]
            kc = jnp.concatenate([kc] * (BLOCK // lanes), axis=1)
            bias[...] = jnp.where(kc == qcode, 0.0, FAR)
            kpart = kbuf[pl.ds(k0, BLOCK), :]
            for h in range(HEADS):
                s = dot(kpart, qz[h]) + bias[...]
                old = mbuf[h : h + 1, :]
                new = jnp.maximum(old, jnp.max(s, axis=0, keepdims=True))
                p = jnp.exp2((s - new).astype(BF16))
                grow = dot(vbuf[kb, h * VROWS : (h + 1) * VROWS, :], p)
                acc[h] = acc[h] * jnp.exp2(old - new) + grow
                mbuf[h : h + 1, :] = new
            return c

        def key_block_bounded(kb, c):
            k0 = pl.multiple_of(kb * BLOCK, BLOCK)
            kc = kcode[pl.ds(k0, BLOCK), :]
            kc = jnp.concatenate([kc] * (BLOCK // lanes), axis=1)
            keep[...] = jnp.where(kc == qcode, 1.0, 0.0).astype(BF16)
            kpart = kbuf[pl.ds(k0, BLOCK), :]
            wide = jnp.exp2(dot(kpart, jnp.concatenate([qz[h] for h in range(HEADS)], axis=1)))
            parts = [wide[:, h * BLOCK : (h + 1) * BLOCK].astype(BF16) * keep[...] for h in range(HEADS)]
            for h in range(HEADS):
                acc[h] = acc[h] + dot(vbuf[kb, h * VROWS : (h + 1) * VROWS, :], parts[h])
            return c

        kb_low, kb_high = low // BLOCK, (high + BLOCK - 1) // BLOCK

        @pl.when(bound < LIMIT)
        def _():
            lax.fori_loop(kb_low, kb_high, key_block_bounded, 0)

        @pl.when(jnp.logical_not(bound < LIMIT))
        def _():
            mbuf[...] = jnp.full(mbuf.shape, FAR, F32)
            lax.fori_loop(kb_low, kb_high, key_block, 0)

        mixed = jnp.concatenate(
            [acc[h, 0:head, :] / acc[h, head : head + 1, :] for h in range(HEADS)], axis=0
        )
        attended = mixed.T.astype(BF16)
        after = (mine.astype(F32) + dot(attended, wo_ref[...])).astype(BF16)
        pre = dot(layer_norm(after, g2_ref[...]), up_ref[...])
        hidden = (0.5 * pre * (1.0 + lax.erf(pre * math.sqrt(0.5)))).astype(BF16)
        out_ref[pl.ds(start, BLOCK), :] = (after.astype(F32) + dot(hidden, down_ref[...])).astype(BF16)
        return carry

    lax.fori_loop(0, rows // BLOCK, query_block, 0)


def attention(ids, lines, first, last, before, after, g1, wq, wk, wv, wo, g2, up, down):
    rows, channels = 2 * PMAX, first.shape[1]
    total = rows + 2 * PMAX
    vmem = pl.BlockSpec(memory_space=pltpu.VMEM)
    return pl.pallas_call(
        attn_kernel,
        out_shape=jax.ShapeDtypeStruct((rows, channels), BF16),
        in_specs=[pl.BlockSpec(memory_space=pltpu.SMEM)] + [vmem] * 13,
        out_specs=vmem,
        scratch_shapes=[
            pltpu.VMEM((total, channels), BF16),
            pltpu.VMEM((total // BLOCK, HEADS * VROWS, BLOCK), BF16),
            pltpu.VMEM((total, 128), F32),
            pltpu.VMEM((HEADS, channels, BLOCK), BF16),
            pltpu.VMEM((BLOCK, BLOCK), F32),
            pltpu.VMEM((HEADS, BLOCK), F32),
            pltpu.VMEM((HEADS, VROWS, BLOCK), F32),
            pltpu.VMEM((BLOCK, BLOCK), BF16),
            pltpu.VMEM((channels, 128), F32),
            pltpu.VMEM((total // 128, 128), F32),
            pltpu.VMEM((rows, channels), BF16),
        ],
        compiler_params=pltpu.CompilerParams(vmem_limit_bytes=48 * 2**20),
        name="attn",
    )(ids, lines, first, last, before, after, g1, wq, wk, wv, wo, g2, up, down)


def body(
    feats, neighbours, send_rows, patch_ids, conv_weight, norm1_gain, query_weight,
    key_weight, value_weight, out_weight, norm2_gain, up_weight, down_weight,
):
    rows, channels = feats.shape
    peers = lax.axis_size("dev")
    slots = send_rows.shape[1] // peers
    lines = patch_ids.reshape(rows // 128, 128)
    flat = flatten_neighbours(neighbours)
    incoming = exchange(send_rows.reshape(peers * slots), feats, peers)
    both = ("region", "dev")
    table = (feats, incoming.reshape(peers * slots, channels), flat, lines, conv_weight)
    first = conv(*table, 0)
    after = shifted(first, both, -1)
    last = conv(*table, rows - PMAX)
    before = shifted(last, both, 1)
    return attention(
        patch_ids.reshape(1, rows), lines, first, last, before, after,
        norm1_gain.reshape(1, channels), query_weight, key_weight, value_weight, out_weight,
        norm2_gain.reshape(1, channels), up_weight, down_weight,
    )


def solution(mesh):
    both = ("region", "dev")
    in_specs = (P(both, None), P(None, both), P(both, None), P(both)) + (P(),) * 9
    return jax.shard_map(
        body, mesh=mesh, in_specs=in_specs, out_specs=P(both, None), check_vma=False
    )
```
